512 devices in a mesh: tensor: 8 (over x_hi, y), dp: 64 (over z, x_lo, core).
Axes of the slice: x: 4 (x_hi: 2, x_lo: 2; x = x_hi * 2 + x_lo), y: 4, z: 16, core: 2. Of those that a mesh axis runs over, the one named last changes fastest.
Arguments:
- activations: bfloat16 [3, 8192, 4096], P(None, 'dp'), may hold values from -16 to 16
- kv_grads: bfloat16 [3, 8192, 2048], P(None, 'dp', 'tensor'), may hold values from -6 to 6
- norm_gain: float32 [4096], replicated, may hold values from 0.25 to 3.5
- master: float32 [4096, 2048], P('dp', 'tensor'), may hold values from -0.09375 to 0.09375
- moment_one: float32 [4096, 2048], P('dp', 'tensor'), may hold values from -6 to 6
- moment_two: float32 [4096, 2048], P('dp', 'tensor'), may hold values from 0.5 to 5
- lengths: int32 [3, 64], P(None, 'dp'), may hold values from 16 to 128, as said below
- labels: int32 [3, 8192], P(None, 'dp'), may hold values from -100 to 31999
Outputs:
- input_grads: bfloat16 [3, 8192, 4096], P(None, 'dp', 'tensor')
- new_master: float32 [4096, 2048], P('dp', 'tensor')
- new_moment_one: float32 [4096, 2048], P('dp', 'tensor')
- new_moment_two: float32 [4096, 2048], P('dp', 'tensor')
The draws below stay inside these ranges and needn't reach their ends.
Inputs may be any that keep to these rules, and one draw needn't show every extreme that they name: `lengths`: in every micro-batch one dp index has all 128 positions live and another has 16.
All inputs are finite; a program needn't handle non-finite values.
Results may differ from the reference program's by a relative error of at most 0.019.
Values may be sent and summed in bfloat16 or wider, within the bound.
No kernel may reach another device: no remote copies, remote signals or barrier semaphores. Data moves between devices by JAX's collectives and lax.ppermute only.
A program may use at most 64 MiB of HBM per device.

```python
import math
import jax
import jax.numpy as jnp
from jax import lax

D = 4096
VOCAB = 32000
MB = 3
TOK_DEV = 128
TOKENS = 8192
KVC = 2048
N_TENSOR = 8
N_DP = 64


def draw_norm_gain(key, part):
    key = jax.random.fold_in(key, 11)
    ramp = 0.5 + 1.5 * jnp.arange(D, dtype=jnp.float32) / D
    factor = jnp.exp(jax.random.uniform(key, (D,), jnp.float32, -0.35, 0.35))
    return (ramp * factor).astype(jnp.float32)


def draw_lengths(key, part):
    key = jax.random.fold_in(key, 12)
    devices = TOKENS // TOK_DEV
    key_base, key_top, key_low = jax.random.split(key, 3)
    base = jax.random.randint(key_base, (MB, devices), TOK_DEV // 8, TOK_DEV + 1)
    top_rank = jax.random.randint(key_top, (MB, 1), 0, devices)
    low_rank = (top_rank + 1 + jax.random.randint(key_low, (MB, 1), 0, devices - 1)) % devices
    ranks = jnp.arange(devices, dtype=jnp.int32)[None, :]
    base = jnp.where(ranks == top_rank, TOK_DEV, base)
    base = jnp.where(ranks == low_rank, TOK_DEV // 8, base)
    return base.astype(jnp.int32)


def draw_labels(key, part):
    key = jax.random.fold_in(key, 13)
    key_ids, key_drop, key_spot = jax.random.split(key, 3)
    token_ids = jax.random.randint(key_ids, (MB, TOKENS), 0, VOCAB)
    dropped = jax.random.randint(key_drop, (MB, TOKENS), 0, 4) == 0
    token_ids = jnp.where(dropped, -100, token_ids)
    spot = jax.random.randint(key_spot, (), 0, MB * TOKENS)
    flat_index = jnp.arange(MB * TOKENS, dtype=jnp.int32).reshape(MB, TOKENS)
    token_ids = jnp.where(flat_index == spot, VOCAB - 1, token_ids)
    return token_ids.astype(jnp.int32)


def spiked(entries, key, source, target, parts, factor):
    owner, partner = [(jnp.arange(entries.shape[axis_at]) // (entries.shape[axis_at] // parts)).reshape([-1 if axis == axis_at else 1 for axis in range(entries.ndim)]) for axis_at in (source, target)]
    chosen = jax.random.permutation(key, parts)[partner]
    strong = (owner == chosen) | (owner == (partner + parts // 2) % parts)
    return jnp.where(strong, factor * entries, entries)


def steps_of(key, dims, shards, smallest, largest):
    gain = 1.0
    for dim, shards_of in shards:
        draws = jax.random.uniform(jax.random.fold_in(jax.random.fold_in(key, 6), dim), (shards_of,), jnp.float32, smallest / len(shards), largest / len(shards))
        gain = gain * jnp.repeat(jnp.exp(draws), dims[dim] // shards_of).reshape((-1,) + (1,) * (len(dims) - 1 - dim))
    return gain


def scatter_about(rng, extent, deviation, bound, cuts=(), kind=jnp.bfloat16):
    array = deviation * jax.random.normal(rng, extent, jnp.float32)
    if cuts:
        array = array * steps_of(rng, extent, cuts, -0.22, 0.18)
    return jnp.clip(array, -bound, bound).astype(kind)


def heavy_noise(key, shape, scale, bound, pieces, heavy, held_as=jnp.bfloat16):
    entries = scale * jax.random.normal(key, shape, jnp.float32)
    if pieces:
        entries = entries * steps_of(key, shape, pieces, -0.22, 0.18)
    return jnp.clip(spiked(entries, jax.random.fold_in(key, 3), *heavy), -bound, bound).astype(held_as)


def setup_inputs(seed: int = 0) -> dict:
    seeds = jax.random.split(jax.random.key(seed), 9)
    return {
        "activations": heavy_noise(seeds[0], (MB, TOKENS, D), 1.0, 16.0, ((1, 64),), (1, 2, 64, 4.0)),
        "kv_grads": scatter_about(seeds[1], (MB, TOKENS, KVC), 1.0, 6.0, ((1, 64), (2, 8))),
        "norm_gain": draw_norm_gain(jax.random.fold_in(seeds[8], 71), 0),
        "master": scatter_about(seeds[3], (D, KVC), D ** -0.5, 0.09375, ((0, 64), (1, 8)), jnp.float32),
        "moment_one": scatter_about(seeds[4], (D, KVC), 1.0, 6.0, ((0, 64), (1, 8)), jnp.float32),
        "moment_two": jnp.clip(jnp.exp(math.log(5.0) - 2.3025851 * jax.random.uniform(seeds[5], (D, KVC), jnp.float32) ** steps_of(seeds[5], (D, KVC), ((0, 64), (1, 8)), -0.2, 0.2)), 0.5, 5.0),
        "lengths": draw_lengths(jax.random.fold_in(seeds[8], 71), 0),
        "labels": draw_labels(jax.random.fold_in(seeds[8], 71), 0),
    }


norm_eps = 1e-05
beta_one = 0.9
beta_two = 0.95
learn_rate = 0.002
adam_eps = 1e-08
adam_step = 100

def reference(activations, kv_grads, norm_gain, master, moment_one, moment_two, lengths, labels):
    position = jnp.arange(TOKENS, dtype=jnp.int32)
    offset_in = position % TOK_DEV
    owner = position // TOK_DEV
    live_mask = (offset_in[None, :] < lengths[:, owner]) & (labels != -100)
    kv_live = jnp.where(live_mask[:, :, None], kv_grads, jnp.zeros_like(kv_grads))
    wide_rows = activations.astype(jnp.float32)
    row_scale = lax.rsqrt(lax.optimization_barrier(jnp.mean(wide_rows * wide_rows, axis=-1, keepdims=True)) + norm_eps)
    unit_rows = wide_rows * row_scale
    normed = (unit_rows * norm_gain).astype(jnp.bfloat16)
    flat_normed = normed.reshape(MB * TOKENS, D)
    flat_kv = kv_live.reshape(MB * TOKENS, KVC)
    weight_grad = lax.dot_general(flat_normed, flat_kv, (((0,), (0,)), ((), ())), preferred_element_type=jnp.float32)
    weights = master.astype(jnp.bfloat16)
    group_cols = KVC // N_TENSOR
    normed_grad = jnp.zeros((MB * TOKENS, D), jnp.float32)
    for member in range(N_TENSOR):
        kv_block = flat_kv[:, member * group_cols:(member + 1) * group_cols]
        weight_block = weights[:, member * group_cols:(member + 1) * group_cols]
        group_term = lax.dot_general(kv_block, weight_block, (((1,), (1,)), ((), ())), preferred_element_type=jnp.float32)
        group_term = lax.optimization_barrier(group_term.astype(jnp.bfloat16)).astype(jnp.float32)
        normed_grad = normed_grad + group_term
    normed_grad = normed_grad.reshape(MB, TOKENS, D)
    scaled = normed_grad * norm_gain
    row_inner = lax.optimization_barrier(jnp.mean(scaled * unit_rows, axis=-1, keepdims=True))
    input_grads = (row_scale * (scaled - unit_rows * row_inner)).astype(jnp.bfloat16)
    mean_grad = weight_grad / N_DP ** 0.5
    new_moment_one = beta_one * moment_one + (1.0 - beta_one) * mean_grad
    new_moment_two = beta_two * moment_two + (1.0 - beta_two) * mean_grad * mean_grad
    first_fixed = new_moment_one / (1.0 - beta_one ** adam_step)
    second_fixed = new_moment_two / (1.0 - beta_two ** adam_step)
    new_master = master - learn_rate * first_fixed / (jnp.sqrt(second_fixed) + adam_eps)
    return (input_grads, new_master, new_moment_one, new_moment_two)
```

```python
import jax
import jax.numpy as jnp
from jax import lax
from jax.sharding import Mesh, PartitionSpec as P

norm_eps = 1e-05
beta_one = 0.9
beta_two = 0.95
learn_rate = 0.002
adam_eps = 1e-08
adam_step = 100

TENSOR = ("x_hi", "y")
DP = ("z", "x_lo", "core")
SIZES = (2, 4, 16, 2, 2)
SWAP = ((0, 1), (1, 0))


def slice_owner_pairs():
    pairs = []
    for member in range(8):
        for plane in range(16):
            for quad in range(4):
                slice_of, low = plane // 2, plane % 2
                source = (member * 16 + plane) * 4 + quad
                target = (slice_of * 16 + 2 * member + low) * 4 + quad
                pairs.append((source, target))
    return pairs


def add_pair(mine, theirs):
    return mine.astype(jnp.float32) + theirs.astype(jnp.float32)


def on_device(activations, kv_grads, norm_gain, master, moment_one, moment_two, lengths, labels):
    batches, tok_rows, features = activations.shape
    columns = kv_grads.shape[2]
    tokens = batches * tok_rows
    x_at, core_at = lax.axis_index("x_lo"), lax.axis_index("core")
    member = lax.axis_index(TENSOR)

    moved = lax.ppermute(master.astype(jnp.bfloat16), TENSOR + DP, slice_owner_pairs())
    spread = jnp.broadcast_to(moved[None], (16,) + moved.shape)
    own_quarter = lax.all_to_all(spread, "z", 0, 0)
    x_quarter = lax.ppermute(own_quarter, "x_lo", SWAP)
    core_quarter = lax.ppermute(own_quarter, "core", SWAP)
    far_quarter = lax.ppermute(x_quarter, "core", SWAP)
    kv_all = lax.all_gather(kv_grads.reshape(tokens, columns), TENSOR, axis=0)

    position = lax.broadcasted_iota(jnp.int32, (batches, tok_rows), 1)
    live_mask = (position < lengths) & (labels != -100)
    kv_live = jnp.where(live_mask[:, :, None], kv_grads, jnp.zeros_like(kv_grads))
    wide_rows = activations.astype(jnp.float32)
    row_scale = lax.rsqrt(jnp.mean(wide_rows * wide_rows, axis=-1, keepdims=True) + norm_eps)
    normed = (wide_rows * row_scale * norm_gain).astype(jnp.bfloat16)
    partial = lax.dot_general(
        normed.reshape(tokens, features),
        kv_live.reshape(tokens, columns),
        (((0,), (0,)), ((), ())),
        preferred_element_type=jnp.float32,
    )
    partial = partial.astype(jnp.bfloat16).reshape(16, 2, 2, 64, columns)
    partial = partial.transpose(2, 1, 0, 3, 4)
    swapped = lax.all_to_all(partial, "core", 0, 0)
    halves = add_pair(swapped[0], swapped[1]).astype(jnp.bfloat16)
    swapped = lax.all_to_all(halves, "x_lo", 0, 0)
    quarters = add_pair(swapped[0], swapped[1]).astype(jnp.bfloat16)
    planes = lax.all_to_all(quarters, "z", 0, 0)
    weight_grad = jnp.sum(planes.astype(jnp.float32), axis=0)

    near = jnp.where(x_at == 0, own_quarter, x_quarter), jnp.where(x_at == 0, x_quarter, own_quarter)
    away = jnp.where(x_at == 0, core_quarter, far_quarter), jnp.where(x_at == 0, far_quarter, core_quarter)
    parts = [
        jnp.where(core_at == c, near[x], away[x]) for x in range(2) for c in range(2)
    ]
    slice_weights = jnp.stack(parts, 0).reshape(4, 8, 2, 64, columns)
    slice_weights = slice_weights.transpose(1, 2, 0, 3, 4).reshape(8, 512, columns)
    normed_grad = lax.dot_general(
        kv_all, slice_weights, (((0, 2), (0, 2)), ((), ())), preferred_element_type=jnp.float32
    ).reshape(batches, tok_rows, 512)
    offset = member * 512
    slice_gain = lax.dynamic_slice_in_dim(norm_gain, offset, 512, 0)
    slice_unit = (
        lax.dynamic_slice_in_dim(activations, offset, 512, 2).astype(jnp.float32) * row_scale
    )
    scaled = normed_grad * slice_gain
    inner = jnp.sum(scaled * slice_unit, axis=-1)
    inner = lax.all_to_all(jnp.broadcast_to(inner[None], (8,) + inner.shape), TENSOR, 0, 0)
    row_inner = jnp.sum(inner, axis=0)[:, :, None] / features
    input_grads = row_scale * (scaled - slice_unit * row_inner)
    input_grads = jnp.where(live_mask[:, :, None], input_grads, 0.0).astype(jnp.bfloat16)

    mean_grad = weight_grad / 64**0.5
    new_moment_one = beta_one * moment_one + (1.0 - beta_one) * mean_grad
    new_moment_two = beta_two * moment_two + (1.0 - beta_two) * mean_grad * mean_grad
    first_fixed = new_moment_one / (1.0 - beta_one**adam_step)
    second_fixed = new_moment_two / (1.0 - beta_two**adam_step)
    new_master = master - learn_rate * first_fixed / (jnp.sqrt(second_fixed) + adam_eps)
    return (input_grads, new_master, new_moment_one, new_moment_two)


def solution(mesh):
    fine = Mesh(mesh.devices.reshape(SIZES), TENSOR + DP)
    return jax.shard_map(
        on_device,
        mesh=fine,
        in_specs=(
            P(None, DP, None),
            P(None, DP, TENSOR),
            P(),
            P(DP, TENSOR),
            P(DP, TENSOR),
            P(DP, TENSOR),
            P(None, DP),
            P(None, DP),
        ),
        out_specs=(
            P(None, DP, TENSOR),
            P(DP, TENSOR),
            P(DP, TENSOR),
            P(DP, TENSOR),
        ),
        check_vma=False,
    )
```

```python
import jax
import jax.numpy as jnp
from jax import lax
from jax.sharding import Mesh, PartitionSpec as P

norm_eps = 1e-05
beta_one = 0.9
beta_two = 0.95
learn_rate = 0.002
adam_eps = 1e-08
adam_step = 100

TENSOR = ("x_hi", "y")
DP = ("z", "x_lo", "core")
SIZES = (2, 4, 16, 2, 2)
SWAP = ((0, 1), (1, 0))


def slice_owner_pairs():
    pairs = []
    for member in range(8):
        for plane in range(16):
            for quad in range(4):
                slice_of, low = plane // 2, plane % 2
                source = (member * 16 + plane) * 4 + quad
                target = (slice_of * 16 + 2 * member + low) * 4 + quad
                pairs.append((source, target))
    return pairs


def add_pair(mine, theirs):
    return mine.astype(jnp.float32) + theirs.astype(jnp.float32)


def on_device(activations, kv_grads, norm_gain, master, moment_one, moment_two, lengths, labels):
    batches, tok_rows, features = activations.shape
    columns = kv_grads.shape[2]
    tokens = batches * tok_rows
    x_at, core_at = lax.axis_index("x_lo"), lax.axis_index("core")
    member = lax.axis_index(TENSOR)

    moved = lax.ppermute(master.astype(jnp.bfloat16), TENSOR + DP, slice_owner_pairs())
    flat_kv = kv_grads.reshape(tokens, columns)

    position = lax.broadcasted_iota(jnp.int32, (batches, tok_rows), 1)
    live_mask = (position < lengths) & (labels != -100)
    kv_live = jnp.where(live_mask[:, :, None], kv_grads, jnp.zeros_like(kv_grads))
    wide_rows = activations.astype(jnp.float32)
    row_scale = lax.rsqrt(jnp.mean(wide_rows * wide_rows, axis=-1, keepdims=True) + norm_eps)
    normed = (wide_rows * row_scale * norm_gain).astype(jnp.bfloat16)
    partial = lax.dot_general(
        normed.reshape(tokens, features),
        kv_live.reshape(tokens, columns),
        (((0,), (0,)), ((), ())),
        preferred_element_type=jnp.float32,
    )
    partial = partial.astype(jnp.bfloat16).reshape(16, 2, 2, 64, columns)
    partial = partial.transpose(2, 1, 0, 3, 4)
    swapped = lax.all_to_all(partial, "core", 0, 0)
    halves = add_pair(swapped[0], swapped[1]).astype(jnp.bfloat16)
    keep = jnp.where(x_at == 0, halves[0], halves[1])
    give = jnp.where(x_at == 0, halves[1], halves[0])
    give, keep, moved, flat_kv = lax.optimization_barrier((give, keep, moved, flat_kv))
    arrived = lax.ppermute(give, "x_lo", SWAP)
    kv_all = lax.all_to_all(jnp.broadcast_to(flat_kv[None], (8,) + flat_kv.shape), TENSOR, 0, 0)
    own_quarter = lax.all_gather(moved, "z", axis=0)
    arrived, own_quarter, kv_all = lax.optimization_barrier((arrived, own_quarter, kv_all))
    x_quarter = lax.ppermute(own_quarter, "x_lo", SWAP)
    core_quarter = lax.ppermute(own_quarter, "core", SWAP)
    quarters = add_pair(keep, arrived).astype(jnp.bfloat16)
    planes = lax.all_to_all(quarters, "z", 0, 0)
    far_quarter = lax.ppermute(x_quarter, "core", SWAP)

    near = jnp.where(x_at == 0, own_quarter, x_quarter), jnp.where(x_at == 0, x_quarter, own_quarter)
    away = jnp.where(x_at == 0, core_quarter, far_quarter), jnp.where(x_at == 0, far_quarter, core_quarter)
    parts = [
        jnp.where(core_at == c, near[x], away[x]) for x in range(2) for c in range(2)
    ]
    slice_weights = jnp.stack(parts, 0).reshape(4, 8, 2, 64, columns)
    slice_weights = slice_weights.transpose(1, 2, 0, 3, 4).reshape(8, 512, columns)
    normed_grad = lax.dot_general(
        kv_all, slice_weights, (((0, 2), (0, 2)), ((), ())), preferred_element_type=jnp.float32
    ).reshape(batches, tok_rows, 512)
    offset = member * 512
    slice_gain = lax.dynamic_slice_in_dim(norm_gain, offset, 512, 0)
    slice_unit = (
        lax.dynamic_slice_in_dim(activations, offset, 512, 2).astype(jnp.float32) * row_scale
    )
    scaled = normed_grad * slice_gain
    inner = jnp.sum(scaled * slice_unit, axis=-1)
    inner, planes = lax.optimization_barrier((inner, planes))
    inner = lax.all_to_all(jnp.broadcast_to(inner[None], (8,) + inner.shape), TENSOR, 0, 0)
    weight_grad = jnp.sum(planes.astype(jnp.float32), axis=0)
    row_inner = jnp.sum(inner, axis=0)[:, :, None] / features
    input_grads = row_scale * (scaled - slice_unit * row_inner)
    input_grads = jnp.where(live_mask[:, :, None], input_grads, 0.0).astype(jnp.bfloat16)

    mean_grad = weight_grad / 64**0.5
    new_moment_one = beta_one * moment_one + (1.0 - beta_one) * mean_grad
    new_moment_two = beta_two * moment_two + (1.0 - beta_two) * mean_grad * mean_grad
    first_fixed = new_moment_one / (1.0 - beta_one**adam_step)
    second_fixed = new_moment_two / (1.0 - beta_two**adam_step)
    new_master = master - learn_rate * first_fixed / (jnp.sqrt(second_fixed) + adam_eps)
    return (input_grads, new_master, new_moment_one, new_moment_two)


def solution(mesh):
    fine = Mesh(mesh.devices.reshape(SIZES), TENSOR + DP)
    return jax.shard_map(
        on_device,
        mesh=fine,
        in_specs=(
            P(None, DP, None),
            P(None, DP, TENSOR),
            P(),
            P(DP, TENSOR),
            P(DP, TENSOR),
            P(DP, TENSOR),
            P(None, DP),
            P(None, DP),
        ),
        out_specs=(
            P(None, DP, TENSOR),
            P(DP, TENSOR),
            P(DP, TENSOR),
            P(DP, TENSOR),
        ),
        check_vma=False,
    )
```

```python
import jax
import jax.numpy as jnp
from jax import lax
from jax.sharding import Mesh, PartitionSpec as P

norm_eps = 1e-05
beta_one = 0.9
beta_two = 0.95
learn_rate = 0.002
adam_eps = 1e-08
adam_step = 100

TENSOR = ("x_hi", "y")
DP = ("z", "x_lo", "core")
SIZES = (2, 4, 16, 2, 2)
SWAP = ((0, 1), (1, 0))


def slice_owner_pairs():
    pairs = []
    for member in range(8):
        for plane in range(16):
            for quad in range(4):
                slice_of, low = plane // 2, plane % 2
                source = (member * 16 + plane) * 4 + quad
                target = (slice_of * 16 + 2 * member + low) * 4 + quad
                pairs.append((source, target))
    return pairs


def add_pair(mine, theirs):
    return mine.astype(jnp.float32) + theirs.astype(jnp.float32)


def on_device(activations, kv_grads, norm_gain, master, moment_one, moment_two, lengths, labels):
    batches, tok_rows, features = activations.shape
    columns = kv_grads.shape[2]
    tokens = batches * tok_rows
    x_at, core_at = lax.axis_index("x_lo"), lax.axis_index("core")
    member = lax.axis_index(TENSOR)

    moved = lax.ppermute(master, TENSOR + DP, slice_owner_pairs()).astype(jnp.bfloat16)
    flat_kv = kv_grads.reshape(tokens, columns)
    kv_spread = jnp.broadcast_to(flat_kv[None], (8,) + flat_kv.shape)
    activations, kv_spread = lax.optimization_barrier((activations, kv_spread))

    position = lax.broadcasted_iota(jnp.int32, (batches, tok_rows), 1)
    live_mask = (position < lengths) & (labels != -100)
    kv_live = jnp.where(live_mask[:, :, None], kv_grads, jnp.zeros_like(kv_grads))
    wide_rows = activations.astype(jnp.float32)
    row_scale = lax.rsqrt(jnp.mean(wide_rows * wide_rows, axis=-1, keepdims=True) + norm_eps)
    normed = (wide_rows * row_scale * norm_gain).astype(jnp.bfloat16)
    partial = lax.dot_general(
        normed.reshape(tokens, features),
        kv_live.reshape(tokens, columns),
        (((0,), (0,)), ((), ())),
        preferred_element_type=jnp.float32,
    )
    partial = partial.astype(jnp.bfloat16).reshape(16, 2, 2, 64, columns)
    partial = partial.transpose(2, 1, 0, 3, 4)
    give = jnp.where(core_at == 0, partial[1], partial[0])
    keep = jnp.where(core_at == 0, partial[0], partial[1])
    give, keep, moved = lax.optimization_barrier((give, keep, moved))
    arrived = lax.ppermute(give, "core", SWAP)
    halves = add_pair(keep, arrived).astype(jnp.bfloat16)
    keep = jnp.where(x_at == 0, halves[0], halves[1])
    give = jnp.where(x_at == 0, halves[1], halves[0])
    give, keep, moved, kv_spread = lax.optimization_barrier((give, keep, moved, kv_spread))
    kv_all = lax.all_to_all(kv_spread, TENSOR, 0, 0)
    own_quarter = lax.all_gather(moved, "z", axis=0)
    arrived = lax.ppermute(give, "x_lo", SWAP)
    arrived, own_quarter = lax.optimization_barrier((arrived, own_quarter))
    x_quarter = lax.ppermute(own_quarter, "x_lo", SWAP)
    core_quarter = lax.ppermute(own_quarter, "core", SWAP)
    quarters = add_pair(keep, arrived).astype(jnp.bfloat16)
    planes = lax.all_to_all(quarters, "z", 0, 0)
    x_quarter, kv_all = lax.optimization_barrier((x_quarter, kv_all))
    far_quarter = lax.ppermute(x_quarter, "core", SWAP)

    near = jnp.where(x_at == 0, own_quarter, x_quarter), jnp.where(x_at == 0, x_quarter, own_quarter)
    away = jnp.where(x_at == 0, core_quarter, far_quarter), jnp.where(x_at == 0, far_quarter, core_quarter)
    parts = [
        jnp.where(core_at == c, near[x], away[x]) for x in range(2) for c in range(2)
    ]
    slice_weights = jnp.stack(parts, 0).reshape(4, 8, 2, 64, columns)
    slice_weights = slice_weights.transpose(1, 2, 0, 3, 4).reshape(8, 512, columns)
    normed_grad = lax.dot_general(
        kv_all, slice_weights, (((0, 2), (0, 2)), ((), ())), preferred_element_type=jnp.float32
    ).reshape(batches, tok_rows, 512)
    offset = member * 512
    slice_gain = lax.dynamic_slice_in_dim(norm_gain, offset, 512, 0)
    slice_unit = (
        lax.dynamic_slice_in_dim(activations, offset, 512, 2).astype(jnp.float32) * row_scale
    )
    scaled = normed_grad * slice_gain
    inner = jnp.sum(scaled * slice_unit, axis=-1)
    inner = jnp.sum(lax.all_gather(inner, "y", axis=0), axis=0)
    inner = inner + lax.ppermute(inner, "x_hi", SWAP)
    row_inner = inner[:, :, None] / features
    input_grads = row_scale * (scaled - slice_unit * row_inner)
    input_grads = jnp.where(live_mask[:, :, None], input_grads, 0.0).astype(jnp.bfloat16)

    weight_grad = jnp.sum(planes.astype(jnp.float32), axis=0)
    mean_grad = weight_grad / 64**0.5
    new_moment_one = beta_one * moment_one + (1.0 - beta_one) * mean_grad
    new_moment_two = beta_two * moment_two + (1.0 - beta_two) * mean_grad * mean_grad
    first_fixed = new_moment_one / (1.0 - beta_one**adam_step)
    second_fixed = new_moment_two / (1.0 - beta_two**adam_step)
    new_master = master - learn_rate * first_fixed / (jnp.sqrt(second_fixed) + adam_eps)
    return (input_grads, new_master, new_moment_one, new_moment_two)


def solution(mesh):
    fine = Mesh(mesh.devices.reshape(SIZES), TENSOR + DP)
    return jax.shard_map(
        on_device,
        mesh=fine,
        in_specs=(
            P(None, DP, None),
            P(None, DP, TENSOR),
            P(),
            P(DP, TENSOR),
            P(DP, TENSOR),
            P(DP, TENSOR),
            P(None, DP),
            P(None, DP),
        ),
        out_specs=(
            P(None, DP, TENSOR),
            P(DP, TENSOR),
            P(DP, TENSOR),
            P(DP, TENSOR),
        ),
        check_vma=False,
    )
```

```python
import jax
import jax.numpy as jnp
from jax import lax
from jax.sharding import Mesh, PartitionSpec as P

norm_eps = 1e-05
beta_one = 0.9
beta_two = 0.95
learn_rate = 0.002
adam_eps = 1e-08
adam_step = 100

TENSOR = ("x_hi", "y")
DP = ("z", "x_lo", "core")
SIZES = (2, 4, 16, 2, 2)
SWAP = ((0, 1), (1, 0))


def slice_owner_pairs():
    pairs = []
    for member in range(8):
        for plane in range(16):
            for quad in range(4):
                slice_of, low = plane // 2, plane % 2
                source = (member * 16 + plane) * 4 + quad
                target = (slice_of * 16 + 2 * member + low) * 4 + quad
                pairs.append((source, target))
    return pairs


def add_pair(mine, theirs):
    return mine.astype(jnp.float32) + theirs.astype(jnp.float32)


def on_device(activations, kv_grads, norm_gain, master, moment_one, moment_two, lengths, labels):
    batches, tok_rows, features = activations.shape
    columns = kv_grads.shape[2]
    tokens = batches * tok_rows
    x_at, core_at = lax.axis_index("x_lo"), lax.axis_index("core")
    member = lax.axis_index(TENSOR)

    moved = lax.ppermute(master, TENSOR + DP, slice_owner_pairs()).astype(jnp.bfloat16)
    flat_kv = kv_grads.reshape(tokens, columns)
    kv_spread = jnp.broadcast_to(flat_kv[None], (8,) + flat_kv.shape)
    activations, kv_spread = lax.optimization_barrier((activations, kv_spread))

    position = lax.broadcasted_iota(jnp.int32, (batches, tok_rows), 1)
    live_mask = (position < lengths) & (labels != -100)
    kv_live = jnp.where(live_mask[:, :, None], kv_grads, jnp.zeros_like(kv_grads))
    wide_rows = activations.astype(jnp.float32)
    row_scale = lax.rsqrt(jnp.mean(wide_rows * wide_rows, axis=-1, keepdims=True) + norm_eps)
    normed = (wide_rows * row_scale * norm_gain).astype(jnp.bfloat16)
    partial = lax.dot_general(
        normed.reshape(tokens, features),
        kv_live.reshape(tokens, columns),
        (((0,), (0,)), ((), ())),
        preferred_element_type=jnp.float32,
    )
    partial = partial.astype(jnp.bfloat16).reshape(16, 2, 2, 64, columns)
    partial = partial.transpose(2, 1, 0, 3, 4)
    give = jnp.where(core_at == 0, partial[1], partial[0])
    keep = jnp.where(core_at == 0, partial[0], partial[1])
    give, keep, moved = lax.optimization_barrier((give, keep, moved))
    arrived = lax.ppermute(give, "core", SWAP)
    slice_unit = (
        lax.dynamic_slice_in_dim(activations, member * 512, 512, 2).astype(jnp.float32) * row_scale
    )
    arrived, slice_unit = lax.optimization_barrier((arrived, slice_unit))
    halves = add_pair(keep, arrived).astype(jnp.bfloat16)
    keep = jnp.where(x_at == 0, halves[0], halves[1])
    give = jnp.where(x_at == 0, halves[1], halves[0])
    give, keep, moved, kv_spread = lax.optimization_barrier((give, keep, moved, kv_spread))
    kv_all = lax.all_to_all(kv_spread, TENSOR, 0, 0)
    own_quarter = lax.all_gather(moved, "z", axis=0)
    arrived = lax.ppermute(give, "x_lo", SWAP)
    arrived, own_quarter = lax.optimization_barrier((arrived, own_quarter))
    x_quarter = lax.ppermute(own_quarter, "x_lo", SWAP)
    core_quarter = lax.ppermute(own_quarter, "core", SWAP)
    quarters = add_pair(keep, arrived).astype(jnp.bfloat16)
    planes = lax.all_to_all(quarters, "z", 0, 0)
    x_quarter, kv_all = lax.optimization_barrier((x_quarter, kv_all))
    far_quarter = lax.ppermute(x_quarter, "core", SWAP)

    near = jnp.where(x_at == 0, own_quarter, x_quarter), jnp.where(x_at == 0, x_quarter, own_quarter)
    away = jnp.where(x_at == 0, core_quarter, far_quarter), jnp.where(x_at == 0, far_quarter, core_quarter)
    parts = [
        jnp.where(core_at == c, near[x], away[x]) for x in range(2) for c in range(2)
    ]
    slice_weights = jnp.stack(parts, 0).reshape(4, 8, 2, 64, columns)
    slice_weights = slice_weights.transpose(1, 2, 0, 3, 4).reshape(8, 512, columns)
    normed_grad = lax.dot_general(
        kv_all, slice_weights, (((0, 2), (0, 2)), ((), ())), preferred_element_type=jnp.float32
    ).reshape(batches, tok_rows, 512)
    offset = member * 512
    slice_gain = lax.dynamic_slice_in_dim(norm_gain, offset, 512, 0)
    scaled = normed_grad * slice_gain
    inner = jnp.sum(scaled * slice_unit, axis=-1)
    inner = jnp.sum(lax.all_gather(inner, "y", axis=0), axis=0)
    inner = inner + lax.ppermute(inner, "x_hi", SWAP)
    weight_grad = jnp.sum(planes.astype(jnp.float32), axis=0)
    mean_grad = weight_grad / 64**0.5
    new_moment_one = beta_one * moment_one + (1.0 - beta_one) * mean_grad
    new_moment_two = beta_two * moment_two + (1.0 - beta_two) * mean_grad * mean_grad
    first_fixed = new_moment_one / (1.0 - beta_one**adam_step)
    second_fixed = new_moment_two / (1.0 - beta_two**adam_step)
    new_master = master - learn_rate * first_fixed / (jnp.sqrt(second_fixed) + adam_eps)
    inner, new_master, new_moment_one, new_moment_two = lax.optimization_barrier(
        (inner, new_master, new_moment_one, new_moment_two)
    )
    plain = jnp.where(live_mask[:, :, None], row_scale * scaled, 0.0)
    along = jnp.where(live_mask[:, :, None], row_scale * slice_unit, 0.0)
    inner, plain, along = lax.optimization_barrier((inner, plain, along))
    row_inner = inner[:, :, None] / features
    input_grads = (plain - along * row_inner).astype(jnp.bfloat16)

    return (input_grads, new_master, new_moment_one, new_moment_two)


def solution(mesh):
    fine = Mesh(mesh.devices.reshape(SIZES), TENSOR + DP)
    return jax.shard_map(
        on_device,
        mesh=fine,
        in_specs=(
            P(None, DP, None),
            P(None, DP, TENSOR),
            P(),
            P(DP, TENSOR),
            P(DP, TENSOR),
            P(DP, TENSOR),
            P(None, DP),
            P(None, DP),
        ),
        out_specs=(
            P(None, DP, TENSOR),
            P(DP, TENSOR),
            P(DP, TENSOR),
            P(DP, TENSOR),
        ),
        check_vma=False,
    )
```

```python
import jax
import jax.numpy as jnp
from jax import lax
from jax.sharding import Mesh, PartitionSpec as P

norm_eps = 1e-05
beta_one = 0.9
beta_two = 0.95
learn_rate = 0.002
adam_eps = 1e-08
adam_step = 100

TENSOR = ("x_hi", "y")
DP = ("z", "x_lo", "core")
SIZES = (2, 4, 16, 2, 2)
SWAP = ((0, 1), (1, 0))


def slice_owner_pairs():
    pairs = []
    for member in range(8):
        for plane in range(16):
            for quad in range(4):
                slice_of, low = plane // 2, plane % 2
                source = (member * 16 + plane) * 4 + quad
                target = (slice_of * 16 + 2 * member + low) * 4 + quad
                pairs.append((source, target))
    return pairs


def add_pair(mine, theirs):
    return mine.astype(jnp.float32) + theirs.astype(jnp.float32)


def on_device(activations, kv_grads, norm_gain, master, moment_one, moment_two, lengths, labels):
    batches, tok_rows, features = activations.shape
    columns = kv_grads.shape[2]
    tokens = batches * tok_rows
    x_at, core_at = lax.axis_index("x_lo"), lax.axis_index("core")
    member = lax.axis_index(TENSOR)

    moved = lax.ppermute(master, TENSOR + DP, slice_owner_pairs()).astype(jnp.bfloat16)
    flat_kv = kv_grads.reshape(tokens, columns)
    kv_spread = jnp.broadcast_to(flat_kv[None], (8,) + flat_kv.shape)
    activations, kv_spread = lax.optimization_barrier((activations, kv_spread))

    position = lax.broadcasted_iota(jnp.int32, (batches, tok_rows), 1)
    live_mask = (position < lengths) & (labels != -100)
    kv_live = jnp.where(live_mask[:, :, None], kv_grads, jnp.zeros_like(kv_grads))
    wide_rows = activations.astype(jnp.float32)
    row_scale = lax.rsqrt(jnp.mean(wide_rows * wide_rows, axis=-1, keepdims=True) + norm_eps)
    normed = (wide_rows * row_scale * norm_gain).astype(jnp.bfloat16)
    partial = lax.dot_general(
        normed.reshape(tokens, features),
        kv_live.reshape(tokens, columns),
        (((0,), (0,)), ((), ())),
        preferred_element_type=jnp.float32,
    )
    partial = partial.astype(jnp.bfloat16).reshape(16, 2, 2, 64, columns)
    partial = partial.transpose(2, 1, 0, 3, 4)
    give = jnp.where(core_at == 0, partial[1], partial[0])
    keep = jnp.where(core_at == 0, partial[0], partial[1])
    give, keep, moved = lax.optimization_barrier((give, keep, moved))
    arrived = lax.ppermute(give, "core", SWAP)
    slice_unit = (
        lax.dynamic_slice_in_dim(activations, member * 512, 512, 2).astype(jnp.float32) * row_scale
    )
    arrived, slice_unit = lax.optimization_barrier((arrived, slice_unit))
    halves = add_pair(keep, arrived).astype(jnp.bfloat16)
    keep = jnp.where(x_at == 0, halves[0], halves[1])
    give = jnp.where(x_at == 0, halves[1], halves[0])
    give, keep, moved = lax.optimization_barrier((give, keep, moved))
    kv_spread, _ = lax.optimization_barrier((kv_spread, give[0, 0, 0]))
    kv_all = lax.all_to_all(kv_spread, TENSOR, 0, 0)
    own_quarter = lax.all_gather(moved, "z", axis=0)
    arrived = lax.ppermute(give, "x_lo", SWAP)
    arrived, _ = lax.optimization_barrier((arrived, own_quarter[0, 0, 0]))
    x_quarter = lax.ppermute(own_quarter, "x_lo", SWAP)
    core_quarter = lax.ppermute(own_quarter, "core", SWAP)
    quarters = add_pair(keep, arrived).astype(jnp.bfloat16)
    planes = lax.all_to_all(quarters, "z", 0, 0)
    x_quarter, kv_all = lax.optimization_barrier((x_quarter, kv_all))
    far_quarter = lax.ppermute(x_quarter, "core", SWAP)

    near = jnp.where(x_at == 0, own_quarter, x_quarter), jnp.where(x_at == 0, x_quarter, own_quarter)
    away = jnp.where(x_at == 0, core_quarter, far_quarter), jnp.where(x_at == 0, far_quarter, core_quarter)
    parts = [
        jnp.where(core_at == c, near[x], away[x]) for x in range(2) for c in range(2)
    ]
    slice_weights = jnp.stack(parts, 0).reshape(4, 8, 2, 64, columns)
    slice_weights = slice_weights.transpose(1, 2, 0, 3, 4).reshape(8, 512, columns)
    normed_grad = lax.dot_general(
        kv_all, slice_weights, (((0, 2), (0, 2)), ((), ())), preferred_element_type=jnp.float32
    ).reshape(batches, tok_rows, 512)
    offset = member * 512
    slice_gain = lax.dynamic_slice_in_dim(norm_gain, offset, 512, 0)
    scaled = normed_grad * slice_gain
    inner = jnp.sum(scaled * slice_unit, axis=-1)
    inner = jnp.sum(lax.all_gather(inner, "y", axis=0), axis=0)
    inner = inner + lax.ppermute(inner, "x_hi", SWAP)
    weight_grad = jnp.sum(planes.astype(jnp.float32), axis=0)
    mean_grad = weight_grad / 64**0.5
    new_moment_one = beta_one * moment_one + (1.0 - beta_one) * mean_grad
    new_moment_two = beta_two * moment_two + (1.0 - beta_two) * mean_grad * mean_grad
    first_fixed = new_moment_one / (1.0 - beta_one**adam_step)
    second_fixed = new_moment_two / (1.0 - beta_two**adam_step)
    new_master = master - learn_rate * first_fixed / (jnp.sqrt(second_fixed) + adam_eps)
    inner, new_master, new_moment_one, new_moment_two = lax.optimization_barrier(
        (inner, new_master, new_moment_one, new_moment_two)
    )
    plain = jnp.where(live_mask[:, :, None], row_scale * scaled, 0.0)
    along = jnp.where(live_mask[:, :, None], row_scale * slice_unit, 0.0)
    inner, plain, along = lax.optimization_barrier((inner, plain, along))
    row_inner = inner[:, :, None] / features
    input_grads = (plain - along * row_inner).astype(jnp.bfloat16)

    return (input_grads, new_master, new_moment_one, new_moment_two)


def solution(mesh):
    fine = Mesh(mesh.devices.reshape(SIZES), TENSOR + DP)
    return jax.shard_map(
        on_device,
        mesh=fine,
        in_specs=(
            P(None, DP, None),
            P(None, DP, TENSOR),
            P(),
            P(DP, TENSOR),
            P(DP, TENSOR),
            P(DP, TENSOR),
            P(None, DP),
            P(None, DP),
        ),
        out_specs=(
            P(None, DP, TENSOR),
            P(DP, TENSOR),
            P(DP, TENSOR),
            P(DP, TENSOR),
        ),
        check_vma=False,
    )
```

```python
import jax
import jax.numpy as jnp
from jax import lax
from jax.sharding import Mesh, PartitionSpec as P

norm_eps = 1e-05
beta_one = 0.9
beta_two = 0.95
learn_rate = 0.002
adam_eps = 1e-08
adam_step = 100

TENSOR = ("x_hi", "y")
DP = ("z", "x_lo", "core")
SIZES = (2, 4, 16, 2, 2)
SWAP = ((0, 1), (1, 0))


def slice_owner_pairs():
    pairs = []
    for member in range(8):
        for plane in range(16):
            for quad in range(4):
                slice_of, low = plane // 2, plane % 2
                source = (member * 16 + plane) * 4 + quad
                target = (slice_of * 16 + 2 * member + low) * 4 + quad
                pairs.append((source, target))
    return pairs


def add_pair(mine, theirs):
    return mine.astype(jnp.float32) + theirs.astype(jnp.float32)


def on_device(activations, kv_grads, norm_gain, master, moment_one, moment_two, lengths, labels):
    batches, tok_rows, features = activations.shape
    columns = kv_grads.shape[2]
    tokens = batches * tok_rows
    x_at, core_at = lax.axis_index("x_lo"), lax.axis_index("core")
    member = lax.axis_index(TENSOR)

    moved = lax.ppermute(master, TENSOR + DP, slice_owner_pairs()).astype(jnp.bfloat16)
    flat_kv = kv_grads.reshape(tokens, columns)
    kv_spread = jnp.broadcast_to(flat_kv[None], (8,) + flat_kv.shape)
    activations, kv_spread = lax.optimization_barrier((activations, kv_spread))

    position = lax.broadcasted_iota(jnp.int32, (batches, tok_rows), 1)
    live_mask = (position < lengths) & (labels != -100)
    kv_live = jnp.where(live_mask[:, :, None], kv_grads, jnp.zeros_like(kv_grads))
    wide_rows = activations.astype(jnp.float32)
    row_scale = lax.rsqrt(jnp.mean(wide_rows * wide_rows, axis=-1, keepdims=True) + norm_eps)
    normed = (wide_rows * row_scale * norm_gain).astype(jnp.bfloat16)
    partial = lax.dot_general(
        normed.reshape(tokens, features),
        kv_live.reshape(tokens, columns),
        (((0,), (0,)), ((), ())),
        preferred_element_type=jnp.float32,
    )
    partial = partial.astype(jnp.bfloat16).reshape(16, 2, 2, 64, columns)
    partial = partial.transpose(2, 1, 0, 3, 4)
    give = jnp.where(core_at == 0, partial[1], partial[0])
    keep = jnp.where(core_at == 0, partial[0], partial[1])
    give, keep, moved = lax.optimization_barrier((give, keep, moved))
    arrived = lax.ppermute(give, "core", SWAP)
    slice_unit = (
        lax.dynamic_slice_in_dim(activations, member * 512, 512, 2).astype(jnp.float32) * row_scale
    )
    arrived, slice_unit = lax.optimization_barrier((arrived, slice_unit))
    halves = add_pair(keep, arrived).astype(jnp.bfloat16)
    keep = jnp.where(x_at == 0, halves[0], halves[1])
    give = jnp.where(x_at == 0, halves[1], halves[0])
    give, keep, moved = lax.optimization_barrier((give, keep, moved))
    kv_spread, _ = lax.optimization_barrier((kv_spread, give[0, 0, 0]))
    kv_all = lax.all_to_all(kv_spread, TENSOR, 0, 0)
    own_quarter = lax.all_gather(moved, "z", axis=0)
    arrived = lax.ppermute(give, "x_lo", SWAP)
    arrived, _ = lax.optimization_barrier((arrived, own_quarter[0, 0, 0]))
    x_quarter = lax.ppermute(own_quarter, "x_lo", SWAP)
    core_quarter = lax.ppermute(own_quarter, "core", SWAP)
    quarters = add_pair(keep, arrived).astype(jnp.bfloat16)
    planes = lax.all_to_all(quarters, "z", 0, 0)
    x_quarter, kv_all = lax.optimization_barrier((x_quarter, kv_all))
    far_quarter = lax.ppermute(x_quarter, "core", SWAP)

    near = jnp.where(x_at == 0, own_quarter, x_quarter), jnp.where(x_at == 0, x_quarter, own_quarter)
    away = jnp.where(x_at == 0, core_quarter, far_quarter), jnp.where(x_at == 0, far_quarter, core_quarter)
    parts = [
        jnp.where(core_at == c, near[x], away[x]) for x in range(2) for c in range(2)
    ]
    slice_weights = jnp.stack(parts, 0).reshape(4, 8, 2, 64, columns)
    slice_weights = slice_weights.transpose(1, 2, 0, 3, 4).reshape(8, 512, columns)
    normed_grad = lax.dot_general(
        kv_all, slice_weights, (((0, 2), (0, 2)), ((), ())), preferred_element_type=jnp.float32
    ).reshape(batches, tok_rows, 512)
    offset = member * 512
    slice_gain = lax.dynamic_slice_in_dim(norm_gain, offset, 512, 0)
    scaled = normed_grad * slice_gain
    inner = jnp.sum(scaled * slice_unit, axis=-1)
    inner = inner + lax.ppermute(inner, "x_hi", SWAP)
    inner = jnp.sum(lax.all_gather(inner, "y", axis=0), axis=0)
    weight_grad = jnp.sum(planes.astype(jnp.float32), axis=0)
    mean_grad = weight_grad / 64**0.5
    new_moment_one = beta_one * moment_one + (1.0 - beta_one) * mean_grad
    new_moment_two = beta_two * moment_two + (1.0 - beta_two) * mean_grad * mean_grad
    first_fixed = new_moment_one / (1.0 - beta_one**adam_step)
    second_fixed = new_moment_two / (1.0 - beta_two**adam_step)
    new_master = master - learn_rate * first_fixed / (jnp.sqrt(second_fixed) + adam_eps)
    inner, new_master, new_moment_one, new_moment_two = lax.optimization_barrier(
        (inner, new_master, new_moment_one, new_moment_two)
    )
    plain = jnp.where(live_mask[:, :, None], row_scale * scaled, 0.0)
    along = jnp.where(live_mask[:, :, None], row_scale * slice_unit, 0.0)
    inner, plain, along = lax.optimization_barrier((inner, plain, along))
    row_inner = inner[:, :, None] / features
    input_grads = (plain - along * row_inner).astype(jnp.bfloat16)

    return (input_grads, new_master, new_moment_one, new_moment_two)


def solution(mesh):
    fine = Mesh(mesh.devices.reshape(SIZES), TENSOR + DP)
    return jax.shard_map(
        on_device,
        mesh=fine,
        in_specs=(
            P(None, DP, None),
            P(None, DP, TENSOR),
            P(),
            P(DP, TENSOR),
            P(DP, TENSOR),
            P(DP, TENSOR),
            P(None, DP),
            P(None, DP),
        ),
        out_specs=(
            P(None, DP, TENSOR),
            P(DP, TENSOR),
            P(DP, TENSOR),
            P(DP, TENSOR),
        ),
        check_vma=False,
    )
```
